512 devices in a mesh: dp: 64 (over z_hi, y, x, core), mp: 8 (over z_lo).
Axes of the slice: x: 4, y: 4, z: 16 (z_hi: 2, z_lo: 8; z = z_hi * 8 + z_lo), core: 2. Of those that a mesh axis runs over, the one named last changes fastest.
Arguments:
- image_feats: bfloat16 [8192, 1792], P('dp'), may hold values from -6 to 6
- text_feats: bfloat16 [8192, 2048], P('dp'), may hold values from -6 to 6
- image_proj: bfloat16 [1792, 1152], P('mp'), may hold values from -0.125 to 0.125
- text_proj: bfloat16 [2048, 1152], P('mp'), may hold values from -0.125 to 0.125
- log_scale: float32 [1], replicated, may hold values from 2 to 2.8
- logit_bias: float32 [1], replicated, may hold values from -7 to -4
Outputs:
- grad_image: float32 [1792, 1152], P('mp')
- grad_text: float32 [2048, 1152], P('mp')
The draws below stay inside these ranges and needn't reach their ends.
All inputs are finite; a program needn't handle non-finite values.
Results may differ from the reference program's by a relative error of at most 0.004.
Values may be sent and summed in bfloat16 or wider, within the bound.
A program may use at most 64 MiB of HBM per device.

```python
import jax
import jax.numpy as jnp
from jax import lax

D_IMAGE = 1792
D_TEXT = 2048
EMBED = 1152
TOK_DEV = 128
TOKENS = 8192


def block_scale(key, extent, cuts, smallest, top_value):
    loudness = 1.0
    for position, blocks in cuts:
        draws = jax.random.uniform(jax.random.fold_in(jax.random.fold_in(key, 6), position), (blocks,), jnp.float32, smallest / len(cuts), top_value / len(cuts))
        loudness = loudness * jnp.repeat(jnp.exp(draws), extent[position] // blocks).reshape((-1,) + (1,) * (len(extent) - 1 - position))
    return loudness


def centred(key, extent, deviation, reach, shards=(), held_as=jnp.bfloat16):
    entries = deviation * jax.random.normal(key, extent, jnp.float32)
    if shards:
        entries = entries * block_scale(key, extent, shards, -0.22, 0.18)
    return jnp.clip(entries, -reach, reach).astype(held_as)


def setup_inputs(seed: int = 0) -> dict:
    arg_keys = jax.random.split(jax.random.key(seed), 7)
    return {
        "image_feats": centred(arg_keys[0], (TOKENS, D_IMAGE), 1.0, 6.0, ((0, 64),)),
        "text_feats": centred(arg_keys[1], (TOKENS, D_TEXT), 1.0, 6.0, ((0, 64),)),
        "image_proj": centred(arg_keys[2], (D_IMAGE, EMBED), D_IMAGE ** -0.5, 0.125, ((0, 8),)),
        "text_proj": centred(arg_keys[3], (D_TEXT, EMBED), D_TEXT ** -0.5, 0.125, ((0, 8),)),
        "log_scale": jnp.clip(jax.random.uniform(arg_keys[4], (1,), jnp.float32, 2.0, 2.8), 2.0, 2.8),
        "logit_bias": jnp.clip(jax.random.uniform(arg_keys[5], (1,), jnp.float32, -7.0, -4.0), -7.0, -4.0),
    }


norm_eps = 1e-06

def pair_weights(left_rows, right_rows, left_ids, right_ids, scale_value, bias_value):
    logits = scale_value * lax.dot_general(left_rows, right_rows, (((1,), (1,)), ((), ())), preferred_element_type=jnp.float32) + bias_value
    matched = left_ids[:, None] == right_ids[None, :]
    slopes = jnp.where(matched, -jax.nn.sigmoid(-logits), jax.nn.sigmoid(logits))
    return (scale_value * slopes).astype(jnp.bfloat16)

def normalize(features, projection):
    pre_rows = jnp.dot(features, projection, preferred_element_type=jnp.float32)
    inverse = lax.rsqrt(lax.optimization_barrier(jnp.sum(pre_rows * pre_rows, 1)) + norm_eps)
    return (pre_rows * inverse[:, None], inverse)

def backward(grads, unit_rows, inverse, features):
    row_dots = lax.optimization_barrier(jnp.sum(grads * unit_rows, 1))
    back_rows = (inverse[:, None] * (grads - unit_rows * row_dots[:, None])).astype(jnp.bfloat16)
    return jnp.dot(features.T, back_rows, preferred_element_type=jnp.float32)

def reference(image_feats, text_feats, image_proj, text_proj, log_scale, logit_bias):
    unit_image, inv_image = normalize(image_feats, image_proj)
    unit_text, inv_text = normalize(text_feats, text_proj)
    emb_image = unit_image.astype(jnp.bfloat16)
    emb_text = unit_text.astype(jnp.bfloat16)
    scale_value = jnp.exp(log_scale[0])
    bias_value = logit_bias[0]
    blocks = TOKENS // TOK_DEV
    text_ids = jnp.arange(TOKENS, dtype=jnp.int32)
    image_blocks = emb_image.reshape(blocks, TOK_DEV, EMBED)

    def one_block(text_grads, inputs):
        image_block, block_index = inputs
        image_ids = block_index * TOK_DEV + jnp.arange(TOK_DEV, dtype=jnp.int32)
        weights = pair_weights(image_block, emb_text, image_ids, text_ids, scale_value, bias_value)
        block_grads = jnp.dot(weights, emb_text, preferred_element_type=jnp.float32)
        text_grads = text_grads + lax.dot_general(weights, image_block, (((0,), (0,)), ((), ())), preferred_element_type=jnp.float32)
        return (text_grads, block_grads)
    dz_text, dz_blocks = lax.scan(one_block, jnp.zeros((TOKENS, EMBED), jnp.float32), (image_blocks, jnp.arange(blocks, dtype=jnp.int32)))
    dz_image = dz_blocks.reshape(TOKENS, EMBED)
    grad_image = backward(dz_image, unit_image, inv_image, image_feats)
    grad_text = backward(dz_text, unit_text, inv_text, text_feats)
    return (grad_image, grad_text)
```

```python
import jax
import jax.numpy as jnp
from jax import lax
from jax.experimental import pallas as pl
from jax.experimental.pallas import tpu as pltpu
from jax.sharding import PartitionSpec as P

norm_eps = 1e-06
f32, bf16 = jnp.float32, jnp.bfloat16
MESH = pl.DeviceIdType.MESH
E = 1152
plane_offsets = [(dx, dy) for dx in range(4) for dy in range(4)]
plane_order = sorted(range(1, 16), key=lambda p: -sum(min(o, 4 - o) for o in plane_offsets[p]))
line_order = [4, 3, 5, 2, 6, 1, 7]


def device_at(x, y, z, c):
    z_hi, z_lo = z // 8, lax.rem(z, 8)
    return {"dp": ((z_hi * 4 + y) * 4 + x) * 2 + c, "mp": z_lo}


def dot(a, b, dims):
    return lax.dot_general(a, b, (dims, ((), ())), preferred_element_type=f32)


def kernel(
    fi, ft, wi, wt, ls, lb, out,
    part, part_in, images, texts, dz_i, dz_t, dz_i_wire, dz_i_in, swap_out, swap_in,
    text_sib_in, dz_t_wire, dz_t_in, back_i, back_t, grads, grads_sib_in, grads_wire,
    grads_in, zsum_out, zsum_in, result,
    s1, r1, st, rt, sx, rx, ss, rs, si, ri, sdi, rdi, sdt, rdt, sb, rb, sg, rg, so, ro, sm, rm,
):
    d, z_lo = lax.axis_index("dp"), lax.axis_index("mp")
    c, x, y, z_hi = lax.rem(d, 2), lax.rem(d // 2, 4), lax.rem(d // 8, 4), d // 32
    z = z_hi * 8 + z_lo
    sibling = device_at(x, y, z, 1 - c)
    pair = device_at(x, y, z + 1 - 2 * lax.rem(z, 2), c)
    far = device_at(x, y, lax.rem(z + 8, 16), c)

    def line(j):
        return device_at(x, y, z_hi * 8 + lax.rem(z_lo + j, 8), c)

    def stride(k):
        return device_at(x, y, lax.rem(z + 2 * k, 16), c)

    def plane(p):
        dx, dy = plane_offsets[p]
        return device_at(lax.rem(x + dx, 4), lax.rem(y + dy, 4), z, c)

    def plane_back(p):
        dx, dy = plane_offsets[p]
        return device_at(lax.rem(x + 4 - dx, 4), lax.rem(y + 4 - dy, 4), z, c)

    def plane_index(p):
        dx, dy = plane_offsets[p]
        return lax.rem(x + dx, 4) * 4 + lax.rem(y + dy, 4)

    def send(src, dst, s, r, to):
        cp = pltpu.make_async_remote_copy(
            src_ref=src, dst_ref=dst, send_sem=s, recv_sem=r, device_id=to, device_id_type=MESH
        )
        cp.start()
        return cp

    partners = [line(j) for j in range(1, 8)]
    partners += [device_at(x, y, (1 - z_hi) * 8 + lax.rem(z_lo + 2 * j, 8), c) for j in range(4)]
    partners += [plane(p) for p in range(1, 16)] + [sibling]
    barrier = pltpu.get_barrier_semaphore()
    for to in partners:
        pl.semaphore_signal(barrier, inc=1, device_id=to, device_id_type=MESH)

    part[:, :E] = dot(fi[:, :224], wi[...], ((1,), (0,))).astype(part.dtype)
    part[:, E:] = dot(ft[...], wt[...], ((1,), (0,))).astype(part.dtype)
    pl.semaphore_wait(barrier, len(partners))

    sends = []
    for j in line_order:
        rows = pl.ds(pl.multiple_of(lax.rem(z_lo + j, 8) * 16, 16), 16)
        sends.append(send(part.at[rows], part_in.at[j - 1], s1.at[j - 1], r1.at[j - 1], line(j)))
    pre = part[pl.ds(pl.multiple_of(z_lo * 16, 16), 16), :].astype(f32)
    for cp in sends:
        cp.wait()
    for j in range(7):
        pre = pre + part_in[j].astype(f32)

    pre_i, pre_t = pre[:, :E], pre[:, E:]
    inv_i = lax.rsqrt(jnp.sum(pre_i * pre_i, 1, keepdims=True) + norm_eps)
    inv_t = lax.rsqrt(jnp.sum(pre_t * pre_t, 1, keepdims=True) + norm_eps)
    unit_i, unit_t = pre_i * inv_i, pre_t * inv_t
    images[0:16, :] = unit_i.astype(bf16)
    texts[0:16, :] = unit_t.astype(bf16)

    swap = send(images.at[pl.ds(0, 16)], images.at[pl.ds(16, 16)], sx.at[0], rx.at[0], pair)
    tsends = {}
    for k in line_order:
        tsends[k] = send(texts.at[pl.ds(0, 16)], texts.at[pl.ds(16 * k, 16)], st.at[k], rt.at[k], stride(k))
    sib = [send(texts.at[pl.ds(0, 16)], texts.at[pl.ds(128, 16)], ss.at[0], rs.at[0], sibling)]
    isends = []
    for p in plane_order:
        isends.append(send(images.at[pl.ds(0, 16)], images.at[pl.ds(32 * p, 16)], si.at[0, p], ri.at[0, p], plane(p)))
    swap.wait()
    for p in plane_order:
        isends.append(send(images.at[pl.ds(16, 16)], images.at[pl.ds(32 * p + 16, 16)], si.at[1, p], ri.at[1, p], plane(p)))
    for k in (1, 7, 2, 6, 3, 5, 4):
        tsends[k].wait()
        sib.append(send(texts.at[pl.ds(16 * k, 16)], texts.at[pl.ds(128 + 16 * k, 16)], ss.at[k], rs.at[k], sibling))
    for cp in sib + isends:
        cp.wait()

    scale = jnp.exp(jnp.full((8, 128), ls[0], f32))[0:1, 0:1]
    bias = lb[0]
    dz_t[...] = jnp.zeros_like(dz_t)

    def chunk(i, carry):
        rows = pl.ds(pl.multiple_of(i * 128, 128), 128)
        mine, every = images[rows, :], texts[...]
        logits = scale * dot(mine, every, ((1,), (1,))) + bias
        row = lax.broadcasted_iota(jnp.int32, (128, 256), 0) + i * 128
        col = lax.broadcasted_iota(jnp.int32, (128, 256), 1)
        matched = (row == col) & (row < 16)
        sig = jax.nn.sigmoid(jnp.where(matched, -logits, logits))
        weights = (scale * jnp.where(matched, -sig, sig)).astype(bf16)
        dz_i[rows, :] = dot(weights, every, ((1,), (0,)))
        dz_t[...] += dot(weights, mine, ((0,), (0,)))
        return carry

    lax.fori_loop(0, 4, chunk, 0)

    tsib = send(dz_t.at[pl.ds(128, 128)], text_sib_in, ss.at[8], rs.at[8], sibling)
    dz_i_wire[...] = dz_i[...].astype(dz_i_wire.dtype)
    dsends = []
    for p in plane_order:
        dsends.append(send(dz_i_wire.at[pl.ds(32 * p, 32)], dz_i_in.at[p], sdi.at[p], rdi.at[p], plane_back(p)))
    tsib.wait()
    dz_text = dz_t[0:128, :] + text_sib_in[...]
    dz_t_wire[...] = dz_text.astype(dz_t_wire.dtype)
    dtsends = []
    for k in line_order:
        dtsends.append(send(dz_t_wire.at[pl.ds(16 * k, 16)], dz_t_in.at[k], sdt.at[k], rdt.at[k], stride(8 - k)))
    sum_i = dz_i[0:32, :]
    for cp in dsends:
        cp.wait()
    for p in range(1, 16):
        sum_i = sum_i + dz_i_in[p].astype(f32)
    swap_out[...] = sum_i[16:32, :]
    swap = send(swap_out, swap_in, sx.at[1], rx.at[1], pair)
    sum_t = dz_text[0:16, :]
    for cp in dtsends:
        cp.wait()
    for k in range(1, 8):
        sum_t = sum_t + dz_t_in[k].astype(f32)
    swap.wait()
    sum_i = sum_i[0:16, :] + swap_in[...]

    dots_i = jnp.sum(sum_i * unit_i, 1, keepdims=True)
    dots_t = jnp.sum(sum_t * unit_t, 1, keepdims=True)
    own = pl.ds(pl.multiple_of(z_lo * 16, 16), 16)
    back_i[own, :] = (inv_i * (sum_i - unit_i * dots_i)).astype(bf16)
    back_t[own, :] = (inv_t * (sum_t - unit_t * dots_t)).astype(bf16)
    bsends = []
    for j in line_order:
        bsends.append(send(back_i.at[own], back_i.at[own], sb.at[0, j - 1], rb.at[0, j - 1], line(j)))
        bsends.append(send(back_t.at[own], back_t.at[own], sb.at[1, j - 1], rb.at[1, j - 1], line(j)))
    for cp in bsends:
        cp.wait()

    grads[0:8] = dot(fi[...], back_i[...], ((0,), (0,))).reshape(8, 32, E)
    grads[8:16] = dot(ft[...], back_t[...], ((0,), (0,))).reshape(8, 32, E)
    give = pl.ds(pl.multiple_of((1 - c) * 16, 16), 16)
    keep = pl.ds(pl.multiple_of(c * 16, 16), 16)
    gsib = send(grads.at[:, give], grads_sib_in, sm.at[0], rm.at[0], sibling)
    gsib.wait()
    me = plane_index(0)

    def add_tile(t, carry):
        grads_wire[t] = (grads[t, keep, :] + grads_sib_in[t]).astype(grads_wire.dtype)
        return carry

    lax.fori_loop(0, 16, add_tile, 0)
    gsends = []
    for p in plane_order:
        gsends.append(send(grads_wire.at[plane_index(p)], grads_in.at[p], sg.at[p], rg.at[p], plane(p)))
    total = grads[me, keep, :] + grads_sib_in[me]
    for cp in gsends:
        cp.wait()
    for p in range(1, 16):
        total = total + grads_in[p].astype(f32)
    zsum_out[...] = total
    zs = send(zsum_out, zsum_in, sm.at[1], rm.at[1], far)
    zs.wait()
    result[me, c] = (total + zsum_in[...]).astype(result.dtype)
    tile = result.at[me, c]
    osends = []
    for p in plane_order:
        osends.append(send(tile, tile, so.at[p], ro.at[p], plane(p)))
    for cp in osends:
        cp.wait()
    whole = send(result.at[:, c], result.at[:, c], sm.at[2], rm.at[2], sibling)
    whole.wait()
    out[...] = result[...].reshape(512, E)


def on_device(image_feats, text_feats, image_proj, text_proj, log_scale, logit_bias):
    m = lax.axis_index("mp")
    fi = jnp.pad(lax.dynamic_slice_in_dim(image_feats, m * 224, 224, 1), ((0, 0), (0, 32)))
    ft = lax.dynamic_slice_in_dim(text_feats, m * 256, 256, 1)
    dma = pltpu.SemaphoreType.DMA
    vmem = pltpu.VMEM
    wire_1, wire_dz, wire_g, wire_o = f32, bf16, bf16, bf16
    grads = pl.pallas_call(
        kernel,
        out_shape=jax.ShapeDtypeStruct((512, E), wire_o),
        in_specs=[pl.BlockSpec(memory_space=vmem)] * 4 + [pl.BlockSpec(memory_space=pltpu.SMEM)] * 2,
        out_specs=pl.BlockSpec(memory_space=vmem),
        scratch_shapes=[
            vmem((128, 2 * E), wire_1), vmem((7, 16, 2 * E), wire_1),
            vmem((512, E), bf16), vmem((256, E), bf16),
            vmem((512, E), f32), vmem((256, E), f32),
            vmem((512, E), wire_dz), vmem((16, 32, E), wire_dz),
            vmem((16, E), f32), vmem((16, E), f32),
            vmem((128, E), f32), vmem((128, E), wire_dz), vmem((8, 16, E), wire_dz),
            vmem((128, E), bf16), vmem((128, E), bf16),
            vmem((16, 32, E), f32), vmem((16, 16, E), f32), vmem((16, 16, E), wire_g),
            vmem((16, 16, E), wire_g), vmem((16, E), f32), vmem((16, E), f32),
            vmem((16, 2, 16, E), wire_o),
            dma((7,)), dma((7,)), dma((8,)), dma((8,)), dma((2,)), dma((2,)), dma((9,)), dma((9,)),
            dma((2, 16)), dma((2, 16)), dma((16,)), dma((16,)), dma((8,)), dma((8,)),
            dma((2, 7)), dma((2, 7)), dma((16,)), dma((16,)), dma((16,)), dma((16,)), dma((3,)), dma((3,)),
        ],
        compiler_params=pltpu.CompilerParams(
            collective_id=0, has_side_effects=True, vmem_limit_bytes=48 * 2**20
        ),
        name="heads",
    )(fi, ft, image_proj, text_proj, log_scale, logit_bias)
    return grads[:224].astype(f32), grads[256:].astype(f32)


def solution(mesh):
    placed = (P("dp", None), P("dp", None), P("mp", None), P("mp", None), P(), P())
    return jax.shard_map(
        on_device,
        mesh=mesh,
        in_specs=placed,
        out_specs=(P("mp", None), P("mp", None)),
        check_vma=False,
    )
```

```python
import jax
import jax.numpy as jnp
from jax import lax
from jax.experimental import pallas as pl
from jax.experimental.pallas import tpu as pltpu
from jax.sharding import PartitionSpec as P

norm_eps = 1e-06
f32, bf16 = jnp.float32, jnp.bfloat16
MESH = pl.DeviceIdType.MESH
E = 1152
plane_offsets = [(dx, dy) for dx in range(4) for dy in range(4)]
plane_order = sorted(range(1, 16), key=lambda p: -sum(min(o, 4 - o) for o in plane_offsets[p]))
line_order = [4, 3, 5, 2, 6, 1, 7]


def device_at(x, y, z, c):
    z_hi, z_lo = z // 8, lax.rem(z, 8)
    return {"dp": ((z_hi * 4 + y) * 4 + x) * 2 + c, "mp": z_lo}


def dot(a, b, dims):
    return lax.dot_general(a, b, (dims, ((), ())), preferred_element_type=f32)


def kernel(
    fi_hbm, ft_hbm, wi_hbm, wt_hbm, ls, lb, out,
    fi, ft, wi, wt, part, acc_1, acc_2, in_1, in_2, in_3,
    images, texts, dz_i, dz_t, dz_i_wire, dz_i_in, swap_out, swap_in,
    text_sib_in, dz_t_wire, dz_t_in, back, grad_i, grads, grads_sib_in, grads_wire,
    grads_in, zsum_out, zsum_in, result,
    sl, s1, r1, st, rt, sx, rx, ss, rs, si, ri, sdi, rdi, sdt, rdt, sb, rb, sg, rg, so, ro, sm, rm,
):
    d, z_lo = lax.axis_index("dp"), lax.axis_index("mp")
    c, x, y, z_hi = lax.rem(d, 2), lax.rem(d // 2, 4), lax.rem(d // 8, 4), d // 32
    z = z_hi * 8 + z_lo
    b0, b1, b2 = lax.rem(z_lo, 2), lax.rem(z_lo // 2, 2), z_lo // 4
    sibling = device_at(x, y, z, 1 - c)
    pair = device_at(x, y, z + 1 - 2 * b0, c)
    two = device_at(x, y, z + 2 - 4 * b1, c)
    four = device_at(x, y, z + 4 - 8 * b2, c)
    far = device_at(x, y, lax.rem(z + 8, 16), c)

    def stride(k):
        return device_at(x, y, lax.rem(z + 2 * k, 16), c)

    def plane(p):
        dx, dy = plane_offsets[p]
        return device_at(lax.rem(x + dx, 4), lax.rem(y + dy, 4), z, c)

    def plane_back(p):
        dx, dy = plane_offsets[p]
        return device_at(lax.rem(x + 4 - dx, 4), lax.rem(y + 4 - dy, 4), z, c)

    def plane_index(p):
        dx, dy = plane_offsets[p]
        return lax.rem(x + dx, 4) * 4 + lax.rem(y + dy, 4)

    def send(src, dst, s, r, to):
        cp = pltpu.make_async_remote_copy(
            src_ref=src, dst_ref=dst, send_sem=s, recv_sem=r, device_id=to, device_id_type=MESH
        )
        cp.start()
        return cp

    partners = [stride(k) for k in line_order] + [pair]
    partners += [plane(p) for p in plane_order] + [sibling]
    barrier = pltpu.get_barrier_semaphore()
    for to in partners:
        pl.semaphore_signal(barrier, inc=1, device_id=to, device_id_type=MESH)

    window = pl.multiple_of(jnp.minimum(z_lo * 224 // 128 * 128, 1408), 128)
    shift = pl.multiple_of(z_lo * 224 - window, 32)
    wi[...] = jnp.zeros_like(wi)
    loads = [
        pltpu.make_async_copy(fi_hbm.at[:, pl.ds(window, 384)], fi, sl.at[0]),
        pltpu.make_async_copy(wi_hbm, wi.at[pl.ds(shift, 224)], sl.at[1]),
        pltpu.make_async_copy(ft_hbm.at[:, pl.ds(pl.multiple_of(z_lo * 256, 256), 256)], ft, sl.at[2]),
        pltpu.make_async_copy(wt_hbm, wt, sl.at[3]),
    ]
    for cp in loads:
        cp.start()
    for cp in loads[:2]:
        cp.wait()
    part[0] = dot(fi[...], wi[...], ((1,), (0,))).reshape(2, 2, 2, 16, E)
    for cp in loads[2:]:
        cp.wait()
    part[1] = dot(ft[...], wt[...], ((1,), (0,))).reshape(2, 2, 2, 16, E)
    pl.semaphore_wait(barrier, len(partners))

    step_1 = [send(part.at[h, :, :, 1 - b0], in_1.at[h], s1.at[h, 0], r1.at[h, 0], pair) for h in range(2)]
    step_2, step_3 = [], []
    for h in range(2):
        step_1[h].wait_recv()
        acc_1[h] = part[h, :, :, b0] + in_1[h]
        step_2.append(send(acc_1.at[h, :, 1 - b1], in_2.at[h], s1.at[h, 1], r1.at[h, 1], two))
    for h in range(2):
        step_2[h].wait_recv()
        acc_2[h] = acc_1[h, :, b1] + in_2[h]
        step_3.append(send(acc_2.at[h, 1 - b2], in_3.at[h], s1.at[h, 2], r1.at[h, 2], four))

    step_3[0].wait_recv()
    pre_i = acc_2[0, b2] + in_3[0]
    inv_i = lax.rsqrt(jnp.sum(pre_i * pre_i, 1, keepdims=True) + norm_eps)
    unit_i = pre_i * inv_i
    images[0:16, :] = unit_i.astype(bf16)
    swap = send(images.at[pl.ds(0, 16)], images.at[pl.ds(16, 16)], sx.at[0], rx.at[0], pair)
    isends = []
    for p in plane_order:
        isends.append(send(images.at[pl.ds(0, 16)], images.at[pl.ds(32 * p, 16)], si.at[0, p], ri.at[0, p], plane(p)))
    step_3[1].wait_recv()
    pre_t = acc_2[1, b2] + in_3[1]
    inv_t = lax.rsqrt(jnp.sum(pre_t * pre_t, 1, keepdims=True) + norm_eps)
    unit_t = pre_t * inv_t
    texts[0:16, :] = unit_t.astype(bf16)
    tsends = {}
    for k in line_order:
        tsends[k] = send(texts.at[pl.ds(0, 16)], texts.at[pl.ds(16 * k, 16)], st.at[k], rt.at[k], stride(k))
    sib = [send(texts.at[pl.ds(0, 16)], texts.at[pl.ds(128, 16)], ss.at[0], rs.at[0], sibling)]
    swap.wait()
    for p in plane_order:
        isends.append(send(images.at[pl.ds(16, 16)], images.at[pl.ds(32 * p + 16, 16)], si.at[1, p], ri.at[1, p], plane(p)))
    for k in (1, 7, 2, 6, 3, 5, 4):
        tsends[k].wait()
        sib.append(send(texts.at[pl.ds(16 * k, 16)], texts.at[pl.ds(128 + 16 * k, 16)], ss.at[k], rs.at[k], sibling))
    for cp in sib + isends:
        cp.wait()
    for cp in step_1 + step_2 + step_3:
        cp.wait_send()

    scale = jnp.exp(jnp.full((8, 128), ls[0], f32))[0:1, 0:1]
    bias = lb[0]
    dz_t[...] = jnp.zeros_like(dz_t)

    def chunk(i, carry):
        rows = pl.ds(pl.multiple_of(i * 128, 128), 128)
        mine, every = images[rows, :], texts[...]
        logits = scale * dot(mine, every, ((1,), (1,))) + bias
        row = lax.broadcasted_iota(jnp.int32, (128, 256), 0) + i * 128
        col = lax.broadcasted_iota(jnp.int32, (128, 256), 1)
        matched = (row == col) & (row < 16)
        sig = jax.nn.sigmoid(jnp.where(matched, -logits, logits))
        weights = (scale * jnp.where(matched, -sig, sig)).astype(bf16)
        dz_i[rows, :] = dot(weights, every, ((1,), (0,)))
        dz_t[...] += dot(weights, mine, ((0,), (0,)))
        return carry

    lax.fori_loop(0, 4, chunk, 0)

    tsib = send(dz_t.at[pl.ds(128, 128)], text_sib_in, ss.at[8], rs.at[8], sibling)
    dz_i_wire[...] = dz_i[...].astype(dz_i_wire.dtype)
    dsends = []
    for p in plane_order:
        dsends.append(send(dz_i_wire.at[pl.ds(32 * p, 32)], dz_i_in.at[p], sdi.at[p], rdi.at[p], plane_back(p)))
    tsib.wait()
    dz_text = dz_t[0:128, :] + text_sib_in[...]
    dz_t_wire[...] = dz_text.astype(dz_t_wire.dtype)
    dtsends = []
    for k in line_order:
        dtsends.append(send(dz_t_wire.at[pl.ds(16 * k, 16)], dz_t_in.at[k], sdt.at[k], rdt.at[k], stride(8 - k)))
    sum_i = dz_i[0:32, :]
    for cp in dsends:
        cp.wait()
    for p in range(1, 16):
        sum_i = sum_i + dz_i_in[p].astype(f32)
    swap_out[...] = sum_i[16:32, :]
    swap = send(swap_out, swap_in, sx.at[1], rx.at[1], pair)
    swap.wait()
    sum_i = sum_i[0:16, :] + swap_in[...]
    dots_i = jnp.sum(sum_i * unit_i, 1, keepdims=True)
    back[0, b2, b1, b0] = (inv_i * (sum_i - unit_i * dots_i)).astype(bf16)

    def spread(h, step):
        block = (
            back.at[h, b2, b1, b0] if step == 0 else back.at[h, :, b1, b0] if step == 1 else back.at[h, :, :, b0]
        )
        return send(block, block, sb.at[h, step], rb.at[h, step], (four, two, pair)[step])

    spreads = [spread(0, 0)]
    sum_t = dz_text[0:16, :]
    for cp in dtsends:
        cp.wait()
    for k in range(1, 8):
        sum_t = sum_t + dz_t_in[k].astype(f32)
    dots_t = jnp.sum(sum_t * unit_t, 1, keepdims=True)
    back[1, b2, b1, b0] = (inv_t * (sum_t - unit_t * dots_t)).astype(bf16)
    spreads.append(spread(1, 0))
    for step in (1, 2):
        for h in range(2):
            spreads[-2].wait_recv()
            spreads.append(spread(h, step))
    spreads[4].wait_recv()
    grad_i[...] = dot(fi[...], back[0].reshape(128, E), ((0,), (0,)))
    for t in range(7):
        grads[t] = grad_i[pl.ds(pl.multiple_of(shift + 32 * t, 32), 32), :]
    grads[7] = jnp.zeros((32, E), f32)
    spreads[5].wait_recv()
    grads[8:16] = dot(ft[...], back[1].reshape(128, E), ((0,), (0,))).reshape(8, 32, E)
    for cp in spreads:
        cp.wait_send()
    give = pl.ds(pl.multiple_of((1 - c) * 16, 16), 16)
    keep = pl.ds(pl.multiple_of(c * 16, 16), 16)
    gsib = send(grads.at[:, give], grads_sib_in, sm.at[0], rm.at[0], sibling)
    gsib.wait()
    me = plane_index(0)

    def add_tile(t, carry):
        grads_wire[t] = (grads[t, keep, :] + grads_sib_in[t]).astype(grads_wire.dtype)
        return carry

    lax.fori_loop(0, 16, add_tile, 0)
    gsends = []
    for p in plane_order:
        gsends.append(send(grads_wire.at[plane_index(p)], grads_in.at[p], sg.at[p], rg.at[p], plane(p)))
    total = grads[me, keep, :] + grads_sib_in[me]
    for cp in gsends:
        cp.wait()
    for p in range(1, 16):
        total = total + grads_in[p].astype(f32)
    zsum_out[...] = total
    zs = send(zsum_out, zsum_in, sm.at[1], rm.at[1], far)
    zs.wait()
    result[me, c] = (total + zsum_in[...]).astype(result.dtype)
    tile = result.at[me, c]
    osends = []
    for p in plane_order:
        osends.append(send(tile, tile, so.at[p], ro.at[p], plane(p)))
    for cp in osends:
        cp.wait()
    whole = send(result.at[:, c], result.at[:, c], sm.at[2], rm.at[2], sibling)
    whole.wait()
    out[...] = result[...].reshape(512, E)


def on_device(image_feats, text_feats, image_proj, text_proj, log_scale, logit_bias):
    dma = pltpu.SemaphoreType.DMA
    vmem = pltpu.VMEM
    wire_dz, wire_g, wire_o = bf16, bf16, bf16
    grads = pl.pallas_call(
        kernel,
        out_shape=jax.ShapeDtypeStruct((512, E), wire_o),
        in_specs=[pl.BlockSpec(memory_space=pl.ANY)] * 4 + [pl.BlockSpec(memory_space=pltpu.SMEM)] * 2,
        out_specs=pl.BlockSpec(memory_space=vmem),
        scratch_shapes=[
            vmem((128, 384), bf16), vmem((128, 256), bf16), vmem((384, E), bf16), vmem((256, E), bf16),
            vmem((2, 2, 2, 2, 16, E), f32), vmem((2, 2, 2, 16, E), f32), vmem((2, 2, 16, E), f32),
            vmem((2, 2, 2, 16, E), f32), vmem((2, 2, 16, E), f32), vmem((2, 16, E), f32),
            vmem((512, E), bf16), vmem((256, E), bf16),
            vmem((512, E), f32), vmem((256, E), f32),
            vmem((512, E), wire_dz), vmem((16, 32, E), wire_dz),
            vmem((16, E), f32), vmem((16, E), f32),
            vmem((128, E), f32), vmem((128, E), wire_dz), vmem((8, 16, E), wire_dz),
            vmem((2, 2, 2, 2, 16, E), bf16), vmem((384, E), f32),
            vmem((16, 32, E), f32), vmem((16, 16, E), f32), vmem((16, 16, E), wire_g),
            vmem((16, 16, E), wire_g), vmem((16, E), f32), vmem((16, E), f32),
            vmem((16, 2, 16, E), wire_o),
            dma((4,)), dma((2, 3)), dma((2, 3)), dma((8,)), dma((8,)), dma((2,)), dma((2,)), dma((9,)), dma((9,)),
            dma((2, 16)), dma((2, 16)), dma((16,)), dma((16,)), dma((8,)), dma((8,)),
            dma((2, 3)), dma((2, 3)), dma((16,)), dma((16,)), dma((16,)), dma((16,)), dma((3,)), dma((3,)),
        ],
        compiler_params=pltpu.CompilerParams(
            collective_id=0, has_side_effects=True, vmem_limit_bytes=48 * 2**20
        ),
        name="heads",
    )(image_feats, text_feats, image_proj, text_proj, log_scale, logit_bias)
    return grads[:224].astype(f32), grads[256:].astype(f32)


def solution(mesh):
    placed = (P("dp", None), P("dp", None), P("mp", None), P("mp", None), P(), P())
    return jax.shard_map(
        on_device,
        mesh=mesh,
        in_specs=placed,
        out_specs=(P("mp", None), P("mp", None)),
        check_vma=False,
    )
```

```python
import jax
import jax.numpy as jnp
from jax import lax
from jax.experimental import pallas as pl
from jax.experimental.pallas import tpu as pltpu
from jax.sharding import PartitionSpec as P

norm_eps = 1e-06
f32, bf16 = jnp.float32, jnp.bfloat16
MESH = pl.DeviceIdType.MESH
E = 1152
plane_offsets = [(dx, dy) for dx in range(4) for dy in range(4)]
plane_order = sorted(range(1, 16), key=lambda p: -sum(min(o, 4 - o) for o in plane_offsets[p]))
line_order = [4, 3, 5, 2, 6, 1, 7]


def device_at(x, y, z, c):
    z_hi, z_lo = z // 8, lax.rem(z, 8)
    return {"dp": ((z_hi * 4 + y) * 4 + x) * 2 + c, "mp": z_lo}


def dot(a, b, dims):
    return lax.dot_general(a, b, (dims, ((), ())), preferred_element_type=f32)


def kernel(
    fi_hbm, ft_hbm, wi_hbm, wt_hbm, ls, lb, out,
    fi, ft, wi, wt, part, part_w, acc_1, acc_1w, acc_2, in_1, in_2, in_3,
    images, texts, dz_i, dz_t, dz_i_wire, dz_i_in, swap_out, swap_in,
    text_sib_in, dz_t_wire, dz_t_in, back, grad_i, grads, grads_sib_in, grads_wire,
    grads_in, zsum_out, zsum_in, result,
    sl, s1, r1, st, rt, sx, rx, ss, rs, si, ri, sdi, rdi, sdt, rdt, sb, rb, sg, rg, so, ro, sm, rm,
):
    d, z_lo = lax.axis_index("dp"), lax.axis_index("mp")
    c, x, y, z_hi = lax.rem(d, 2), lax.rem(d // 2, 4), lax.rem(d // 8, 4), d // 32
    z = z_hi * 8 + z_lo
    b0, b1, b2 = lax.rem(z_lo, 2), lax.rem(z_lo // 2, 2), z_lo // 4
    sibling = device_at(x, y, z, 1 - c)
    pair = device_at(x, y, z + 1 - 2 * b0, c)
    two = device_at(x, y, z + 2 - 4 * b1, c)
    four = device_at(x, y, z + 4 - 8 * b2, c)
    far = device_at(x, y, lax.rem(z + 8, 16), c)

    def stride(k):
        return device_at(x, y, lax.rem(z + 2 * k, 16), c)

    def plane(p):
        dx, dy = plane_offsets[p]
        return device_at(lax.rem(x + dx, 4), lax.rem(y + dy, 4), z, c)

    def plane_back(p):
        dx, dy = plane_offsets[p]
        return device_at(lax.rem(x + 4 - dx, 4), lax.rem(y + 4 - dy, 4), z, c)

    def plane_index(p):
        dx, dy = plane_offsets[p]
        return lax.rem(x + dx, 4) * 4 + lax.rem(y + dy, 4)

    def send(src, dst, s, r, to):
        cp = pltpu.make_async_remote_copy(
            src_ref=src, dst_ref=dst, send_sem=s, recv_sem=r, device_id=to, device_id_type=MESH
        )
        cp.start()
        return cp

    partners = [stride(k) for k in line_order] + [pair]
    partners += [plane(p) for p in plane_order] + [sibling]
    barrier = pltpu.get_barrier_semaphore()
    for to in partners:
        pl.semaphore_signal(barrier, inc=1, device_id=to, device_id_type=MESH)

    window = pl.multiple_of(jnp.minimum(z_lo * 224 // 128 * 128, 1408), 128)
    shift = pl.multiple_of(z_lo * 224 - window, 32)
    wi[...] = jnp.zeros_like(wi)
    loads = [
        pltpu.make_async_copy(fi_hbm.at[:, pl.ds(window, 384)], fi, sl.at[0]),
        pltpu.make_async_copy(wi_hbm, wi.at[pl.ds(shift, 224)], sl.at[1]),
        pltpu.make_async_copy(ft_hbm.at[:, pl.ds(pl.multiple_of(z_lo * 256, 256), 256)], ft, sl.at[2]),
        pltpu.make_async_copy(wt_hbm, wt, sl.at[3]),
    ]
    for cp in loads:
        cp.start()
    for cp in loads[:2]:
        cp.wait()
    part[0] = dot(fi[...], wi[...], ((1,), (0,))).reshape(2, 2, 2, 16, E)
    part_w[0] = part[0].astype(bf16)
    for cp in loads[2:]:
        cp.wait()
    part[1] = dot(ft[...], wt[...], ((1,), (0,))).reshape(2, 2, 2, 16, E)
    part_w[1] = part[1].astype(bf16)
    pl.semaphore_wait(barrier, len(partners))

    step_1 = [send(part_w.at[h, :, :, 1 - b0], in_1.at[h], s1.at[h, 0], r1.at[h, 0], pair) for h in range(2)]
    step_2, step_3 = [], []
    for h in range(2):
        step_1[h].wait_recv()
        acc_1[h] = part[h, :, :, b0] + in_1[h].astype(f32)
        acc_1w[h] = acc_1[h].astype(bf16)
        step_2.append(send(acc_1w.at[h, :, 1 - b1], in_2.at[h], s1.at[h, 1], r1.at[h, 1], two))
    for h in range(2):
        step_2[h].wait_recv()
        acc_2[h] = acc_1[h, :, b1] + in_2[h].astype(f32)
        step_3.append(send(acc_2.at[h, 1 - b2], in_3.at[h], s1.at[h, 2], r1.at[h, 2], four))

    step_3[0].wait_recv()
    pre_i = acc_2[0, b2] + in_3[0]
    inv_i = lax.rsqrt(jnp.sum(pre_i * pre_i, 1, keepdims=True) + norm_eps)
    unit_i = pre_i * inv_i
    images[0:16, :] = unit_i.astype(bf16)
    swap = send(images.at[pl.ds(0, 16)], images.at[pl.ds(16, 16)], sx.at[0], rx.at[0], pair)
    isends = []
    for p in plane_order:
        isends.append(send(images.at[pl.ds(0, 16)], images.at[pl.ds(32 * p, 16)], si.at[0, p], ri.at[0, p], plane(p)))
    step_3[1].wait_recv()
    pre_t = acc_2[1, b2] + in_3[1]
    inv_t = lax.rsqrt(jnp.sum(pre_t * pre_t, 1, keepdims=True) + norm_eps)
    unit_t = pre_t * inv_t
    texts[0:16, :] = unit_t.astype(bf16)
    tsends = {}
    for k in line_order:
        tsends[k] = send(texts.at[pl.ds(0, 16)], texts.at[pl.ds(16 * k, 16)], st.at[k], rt.at[k], stride(k))
    sib = [send(texts.at[pl.ds(0, 16)], texts.at[pl.ds(128, 16)], ss.at[0], rs.at[0], sibling)]
    swap.wait()
    for p in plane_order:
        isends.append(send(images.at[pl.ds(16, 16)], images.at[pl.ds(32 * p + 16, 16)], si.at[1, p], ri.at[1, p], plane(p)))
    for k in (1, 7, 2, 6, 3, 5, 4):
        tsends[k].wait()
        sib.append(send(texts.at[pl.ds(16 * k, 16)], texts.at[pl.ds(128 + 16 * k, 16)], ss.at[k], rs.at[k], sibling))
    for cp in sib + isends:
        cp.wait()
    for cp in step_1 + step_2 + step_3:
        cp.wait_send()

    scale = jnp.exp(jnp.full((8, 128), ls[0], f32))[0:1, 0:1]
    bias = lb[0]

    dsends = []
    for i in (2, 1, 3, 0):
        rows = slice(i * 128, i * 128 + 128)
        mine, every = images[rows, :], texts[...]
        logits = scale * dot(mine, every, ((1,), (1,))) + bias
        if i == 0:
            row = lax.broadcasted_iota(jnp.int32, (128, 256), 0)
            col = lax.broadcasted_iota(jnp.int32, (128, 256), 1)
            matched = (row == col) & (row < 16)
            sig = jax.nn.sigmoid(jnp.where(matched, -logits, logits))
            slopes = jnp.where(matched, -sig, sig)
        else:
            slopes = jax.nn.sigmoid(logits)
        weights = (scale * slopes).astype(bf16)
        dz_rows = dot(weights, every, ((1,), (0,)))
        if i == 0:
            dz_i[...] = dz_rows[0:32]
        dz_i_wire[rows, :] = dz_rows.astype(dz_i_wire.dtype)
        for p in plane_order:
            if p // 4 == i:
                dsends.append(send(dz_i_wire.at[pl.ds(32 * p, 32)], dz_i_in.at[p], sdi.at[p], rdi.at[p], plane_back(p)))
        more = dot(weights, mine, ((0,), (0,)))
        dz_t[...] = more if i == 2 else dz_t[...] + more

    tsib = send(dz_t.at[pl.ds(128, 128)], text_sib_in, ss.at[8], rs.at[8], sibling)
    tsib.wait()
    dz_text = dz_t[0:128, :] + text_sib_in[...]
    dz_t_wire[...] = dz_text.astype(dz_t_wire.dtype)
    dtsends = []
    for k in line_order:
        dtsends.append(send(dz_t_wire.at[pl.ds(16 * k, 16)], dz_t_in.at[k], sdt.at[k], rdt.at[k], stride(8 - k)))
    sum_i = dz_i[0:32, :]
    for cp in dsends:
        cp.wait()
    for p in range(1, 16):
        sum_i = sum_i + dz_i_in[p].astype(f32)
    swap_out[...] = sum_i[16:32, :]
    swap = send(swap_out, swap_in, sx.at[1], rx.at[1], pair)
    swap.wait()
    sum_i = sum_i[0:16, :] + swap_in[...]
    dots_i = jnp.sum(sum_i * unit_i, 1, keepdims=True)
    back[0, b2, b1, b0] = (inv_i * (sum_i - unit_i * dots_i)).astype(bf16)

    def spread(h, step):
        block = (
            back.at[h, b2, b1, b0] if step == 0 else back.at[h, :, b1, b0] if step == 1 else back.at[h, :, :, b0]
        )
        return send(block, block, sb.at[h, step], rb.at[h, step], (four, two, pair)[step])

    spreads = [spread(0, 0)]
    sum_t = dz_text[0:16, :]
    for cp in dtsends:
        cp.wait()
    for k in range(1, 8):
        sum_t = sum_t + dz_t_in[k].astype(f32)
    dots_t = jnp.sum(sum_t * unit_t, 1, keepdims=True)
    back[1, b2, b1, b0] = (inv_t * (sum_t - unit_t * dots_t)).astype(bf16)
    spreads.append(spread(1, 0))
    for step in (1, 2):
        for h in range(2):
            spreads[-2].wait_recv()
            spreads.append(spread(h, step))
    spreads[4].wait_recv()
    give = pl.ds(pl.multiple_of((1 - c) * 16, 16), 16)
    keep = pl.ds(pl.multiple_of(c * 16, 16), 16)
    halves = (pl.ds(0, 8), pl.ds(8, 8))
    grad_i[...] = dot(fi[...], back[0].reshape(128, E), ((0,), (0,)))
    for t in range(7):
        grads[t] = grad_i[pl.ds(pl.multiple_of(shift + 32 * t, 32), 32), :]
    grads[7] = jnp.zeros((32, E), f32)
    gsib = [send(grads.at[halves[0], give], grads_sib_in.at[halves[0]], sm.at[0], rm.at[0], sibling)]
    spreads[5].wait_recv()
    grads[8:16] = dot(ft[...], back[1].reshape(128, E), ((0,), (0,))).reshape(8, 32, E)
    gsib.append(send(grads.at[halves[1], give], grads_sib_in.at[halves[1]], sm.at[1], rm.at[1], sibling))
    for cp in spreads:
        cp.wait_send()

    def add_tile(t, carry):
        grads_wire[t] = (grads[t, keep, :] + grads_sib_in[t]).astype(grads_wire.dtype)
        return carry

    for h in range(2):
        gsib[h].wait()
        lax.fori_loop(8 * h, 8 * h + 8, add_tile, 0)
    me = plane_index(0)
    runs = (slice(0, 640), slice(640, E))
    spans = (pl.ds(0, 640), pl.ds(640, 512))
    gsends, zsends, osends, totals = [], [], [], []
    for h, cols in enumerate(spans):
        gsends.append([
            send(grads_wire.at[plane_index(p), :, cols], grads_in.at[p, :, cols], sg.at[h, p], rg.at[h, p], plane(p))
            for p in plane_order
        ])
    for h, run in enumerate(runs):
        total = grads[me, keep, run] + grads_sib_in[me, :, run]
        for cp in gsends[h]:
            cp.wait_recv()
        for p in range(1, 16):
            total = total + grads_in[p, :, run].astype(f32)
        zsum_out[:, run] = total
        zsends.append(send(zsum_out.at[:, spans[h]], zsum_in.at[:, spans[h]], sm.at[2 + h], rm.at[2 + h], far))
    for h, run in enumerate(runs):
        zsends[h].wait_recv()
        result[me, c, :, run] = (zsum_out[:, run] + zsum_in[:, run]).astype(result.dtype)
        tile = result.at[me, c, :, spans[h]]
        osends.append([send(tile, tile, so.at[h, p], ro.at[h, p], plane(p)) for p in plane_order])
    whole = []
    for h in range(2):
        for cp in osends[h]:
            cp.wait_recv()
        block = result.at[:, c, :, spans[h]]
        whole.append(send(block, block, sm.at[4 + h], rm.at[4 + h], sibling))
    for cp in gsends[0] + gsends[1] + zsends + osends[0] + osends[1]:
        cp.wait_send()
    for cp in whole:
        cp.wait()
    out[...] = result[...].reshape(512, E)


def on_device(image_feats, text_feats, image_proj, text_proj, log_scale, logit_bias):
    dma = pltpu.SemaphoreType.DMA
    vmem = pltpu.VMEM
    wire_dz, wire_g, wire_o = bf16, bf16, bf16
    grads = pl.pallas_call(
        kernel,
        out_shape=jax.ShapeDtypeStruct((512, E), wire_o),
        in_specs=[pl.BlockSpec(memory_space=pl.ANY)] * 4 + [pl.BlockSpec(memory_space=pltpu.SMEM)] * 2,
        out_specs=pl.BlockSpec(memory_space=vmem),
        scratch_shapes=[
            vmem((128, 384), bf16), vmem((128, 256), bf16), vmem((384, E), bf16), vmem((256, E), bf16),
            vmem((2, 2, 2, 2, 16, E), f32), vmem((2, 2, 2, 2, 16, E), bf16),
            vmem((2, 2, 2, 16, E), f32), vmem((2, 2, 2, 16, E), bf16),
            vmem((2, 2, 16, E), f32),
            vmem((2, 2, 2, 16, E), bf16), vmem((2, 2, 16, E), bf16), vmem((2, 16, E), f32),
            vmem((512, E), bf16), vmem((256, E), bf16),
            vmem((32, E), f32), vmem((256, E), f32),
            vmem((512, E), wire_dz), vmem((16, 32, E), wire_dz),
            vmem((16, E), f32), vmem((16, E), f32),
            vmem((128, E), f32), vmem((128, E), wire_dz), vmem((8, 16, E), wire_dz),
            vmem((2, 2, 2, 2, 16, E), bf16), vmem((384, E), f32),
            vmem((16, 32, E), f32), vmem((16, 16, E), f32), vmem((16, 16, E), wire_g),
            vmem((16, 16, E), wire_g), vmem((16, E), f32), vmem((16, E), f32),
            vmem((16, 2, 16, E), wire_o),
            dma((4,)), dma((2, 3)), dma((2, 3)), dma((8,)), dma((8,)), dma((2,)), dma((2,)), dma((9,)), dma((9,)),
            dma((2, 16)), dma((2, 16)), dma((16,)), dma((16,)), dma((8,)), dma((8,)),
            dma((2, 3)), dma((2, 3)), dma((2, 16)), dma((2, 16)), dma((2, 16)), dma((2, 16)), dma((6,)), dma((6,)),
        ],
        compiler_params=pltpu.CompilerParams(
            collective_id=0, has_side_effects=True, vmem_limit_bytes=62 * 2**20
        ),
        name="heads",
    )(image_feats, text_feats, image_proj, text_proj, log_scale, logit_bias)
    return grads[:224].astype(f32), grads[256:].astype(f32)


def solution(mesh):
    placed = (P("dp", None), P("dp", None), P("mp", None), P("mp", None), P(), P())
    return jax.shard_map(
        on_device,
        mesh=mesh,
        in_specs=placed,
        out_specs=(P("mp", None), P("mp", None)),
        check_vma=False,
    )
```

```python
import jax
import jax.numpy as jnp
from jax import lax
from jax.experimental import pallas as pl
from jax.experimental.pallas import tpu as pltpu
from jax.sharding import PartitionSpec as P

norm_eps = 1e-06
f32, bf16 = jnp.float32, jnp.bfloat16
MESH = pl.DeviceIdType.MESH
E = 1152
plane_offsets = [(dx, dy) for dx in range(4) for dy in range(4)]
plane_order = sorted(range(1, 16), key=lambda p: -sum(min(o, 4 - o) for o in plane_offsets[p]))
line_order = [4, 3, 5, 2, 6, 1, 7]


def device_at(x, y, z, c):
    z_hi, z_lo = z // 8, lax.rem(z, 8)
    return {"dp": ((z_hi * 4 + y) * 4 + x) * 2 + c, "mp": z_lo}


def dot(a, b, dims):
    return lax.dot_general(a, b, (dims, ((), ())), preferred_element_type=f32)


def kernel(
    fi_hbm, ft_hbm, wi_hbm, wt_hbm, ls, lb, out,
    fi, ft, wi, wt, part, part_w, acc_1, acc_1w, acc_2, in_1, in_2, in_3,
    images, texts, dz_i, dz_t, dz_i_wire, dz_i_in, swap_out, swap_in,
    text_sib_in, dz_t_wire, dz_t_in, back, grad_i, grads, grads_sib_in, grads_wire,
    grads_in, zsum_out, zsum_in,
    sl, s1, r1, st, rt, sx, rx, ss, rs, si, ri, sdi, rdi, sdt, rdt, sb, rb, sg, rg, so, ro, sm, rm, gate,
):
    d, z_lo = lax.axis_index("dp"), lax.axis_index("mp")
    c, x, y, z_hi = lax.rem(d, 2), lax.rem(d // 2, 4), lax.rem(d // 8, 4), d // 32
    z = z_hi * 8 + z_lo
    b0, b1, b2 = lax.rem(z_lo, 2), lax.rem(z_lo // 2, 2), z_lo // 4
    sibling = device_at(x, y, z, 1 - c)
    pair = device_at(x, y, z + 1 - 2 * b0, c)
    two = device_at(x, y, z + 2 - 4 * b1, c)
    four = device_at(x, y, z + 4 - 8 * b2, c)
    far = device_at(x, y, lax.rem(z + 8, 16), c)

    def stride(k):
        return device_at(x, y, lax.rem(z + 2 * k, 16), c)

    def plane(p):
        dx, dy = plane_offsets[p]
        return device_at(lax.rem(x + dx, 4), lax.rem(y + dy, 4), z, c)

    def plane_back(p):
        dx, dy = plane_offsets[p]
        return device_at(lax.rem(x + 4 - dx, 4), lax.rem(y + 4 - dy, 4), z, c)

    def plane_index(p):
        dx, dy = plane_offsets[p]
        return lax.rem(x + dx, 4) * 4 + lax.rem(y + dy, 4)

    def send(src, dst, s, r, to):
        cp = pltpu.make_async_remote_copy(
            src_ref=src, dst_ref=dst, send_sem=s, recv_sem=r, device_id=to, device_id_type=MESH
        )
        cp.start()
        return cp

    def along(k):
        return device_at(x, y, lax.rem(z + 16 + k, 16), c)

    partners = [along(1), along(-1)] + [plane(p) for p in plane_order] + [sibling]
    barrier = pltpu.get_barrier_semaphore()
    for to in partners:
        pl.semaphore_signal(barrier, inc=1, device_id=to, device_id_type=MESH)

    def greet(r):
        pl.semaphore_signal(gate.at[r, 0], inc=1, device_id=along(2**r), device_id_type=MESH)
        pl.semaphore_signal(gate.at[r, 1], inc=1, device_id=along(-(2**r)), device_id_type=MESH)

    def greeted(r):
        pl.semaphore_wait(gate.at[r, 0], 1)
        pl.semaphore_wait(gate.at[r, 1], 1)

    window = pl.multiple_of(jnp.minimum(z_lo * 224 // 128 * 128, 1408), 128)
    shift = pl.multiple_of(z_lo * 224 - window, 32)
    wi[...] = jnp.zeros_like(wi)
    loads = [
        pltpu.make_async_copy(fi_hbm.at[:, pl.ds(window, 384)], fi, sl.at[0]),
        pltpu.make_async_copy(wi_hbm, wi.at[pl.ds(shift, 224)], sl.at[1]),
        pltpu.make_async_copy(ft_hbm.at[:, pl.ds(pl.multiple_of(z_lo * 256, 256), 256)], ft, sl.at[2]),
        pltpu.make_async_copy(wt_hbm, wt, sl.at[3]),
    ]
    for cp in loads:
        cp.start()
    for cp in loads[:2]:
        cp.wait()
    part[0] = dot(fi[...], wi[...], ((1,), (0,))).reshape(2, 2, 2, 16, E)
    part_w[0] = part[0].astype(bf16)
    for cp in loads[2:]:
        cp.wait()
    part[1] = dot(ft[...], wt[...], ((1,), (0,))).reshape(2, 2, 2, 16, E)
    part_w[1] = part[1].astype(bf16)
    pl.semaphore_wait(barrier, len(partners))
    greet(0)

    step_1 = [send(part_w.at[h, :, :, 1 - b0], in_1.at[h], s1.at[h, 0], r1.at[h, 0], pair) for h in range(2)]
    greeted(0)
    greet(1)
    step_2, step_3 = [], []
    for h in range(2):
        step_1[h].wait_recv()
        acc_1[h] = part[h, :, :, b0] + in_1[h].astype(f32)
        acc_1w[h] = acc_1[h].astype(bf16)
        step_2.append(send(acc_1w.at[h, :, 1 - b1], in_2.at[h], s1.at[h, 1], r1.at[h, 1], two))
    greeted(1)
    greet(2)
    for h in range(2):
        step_2[h].wait_recv()
        acc_2[h] = acc_1[h, :, b1] + in_2[h].astype(f32)
        step_3.append(send(acc_2.at[h, 1 - b2], in_3.at[h], s1.at[h, 2], r1.at[h, 2], four))

    step_3[0].wait_recv()
    pre_i = acc_2[0, b2] + in_3[0]
    inv_i = lax.rsqrt(jnp.sum(pre_i * pre_i, 1, keepdims=True) + norm_eps)
    unit_i = pre_i * inv_i
    images[0:16, :] = unit_i.astype(bf16)
    swap = send(images.at[pl.ds(0, 16)], images.at[pl.ds(16, 16)], sx.at[0], rx.at[0], pair)
    isends = []
    for p in plane_order:
        isends.append(send(images.at[pl.ds(0, 16)], images.at[pl.ds(32 * p, 16)], si.at[0, p], ri.at[0, p], plane(p)))
    step_3[1].wait_recv()
    pre_t = acc_2[1, b2] + in_3[1]
    inv_t = lax.rsqrt(jnp.sum(pre_t * pre_t, 1, keepdims=True) + norm_eps)
    unit_t = pre_t * inv_t
    texts[0:16, :] = unit_t.astype(bf16)
    greeted(2)
    tsends = {}
    for k in line_order:
        tsends[k] = send(texts.at[pl.ds(0, 16)], texts.at[pl.ds(16 * k, 16)], st.at[k], rt.at[k], stride(k))
    sib = [send(texts.at[pl.ds(0, 16)], texts.at[pl.ds(128, 16)], ss.at[0], rs.at[0], sibling)]
    swap.wait()
    for p in plane_order:
        isends.append(send(images.at[pl.ds(16, 16)], images.at[pl.ds(32 * p + 16, 16)], si.at[1, p], ri.at[1, p], plane(p)))
    for k in (1, 7, 2, 6, 3, 5, 4):
        tsends[k].wait()
        sib.append(send(texts.at[pl.ds(16 * k, 16)], texts.at[pl.ds(128 + 16 * k, 16)], ss.at[k], rs.at[k], sibling))
    for cp in sib + isends:
        cp.wait()
    for cp in step_1 + step_2 + step_3:
        cp.wait_send()

    scale = jnp.exp(jnp.full((8, 128), ls[0], f32))[0:1, 0:1]
    bias = lb[0]

    dsends = []
    for i in (2, 1, 3, 0):
        rows = slice(i * 128, i * 128 + 128)
        mine, every = images[rows, :], texts[...]
        logits = scale * dot(mine, every, ((1,), (1,))) + bias
        if i == 0:
            row = lax.broadcasted_iota(jnp.int32, (128, 256), 0)
            col = lax.broadcasted_iota(jnp.int32, (128, 256), 1)
            matched = (row == col) & (row < 16)
            sig = jax.nn.sigmoid(jnp.where(matched, -logits, logits))
            slopes = jnp.where(matched, -sig, sig)
        else:
            slopes = jax.nn.sigmoid(logits)
        weights = (scale * slopes).astype(bf16)
        dz_rows = dot(weights, every, ((1,), (0,)))
        if i == 0:
            dz_i[...] = dz_rows[0:32]
        dz_i_wire[rows, :] = dz_rows.astype(dz_i_wire.dtype)
        for p in plane_order:
            if p // 4 == i:
                dsends.append(send(dz_i_wire.at[pl.ds(32 * p, 32)], dz_i_in.at[p], sdi.at[p], rdi.at[p], plane_back(p)))
        more = dot(weights, mine, ((0,), (0,)))
        dz_t[...] = more if i == 2 else dz_t[...] + more

    tsib = send(dz_t.at[pl.ds(128, 128)], text_sib_in, ss.at[8], rs.at[8], sibling)
    tsib.wait()
    dz_text = dz_t[0:128, :] + text_sib_in[...]
    dz_t_wire[...] = dz_text.astype(dz_t_wire.dtype)
    dtsends = []
    for k in line_order:
        dtsends.append(send(dz_t_wire.at[pl.ds(16 * k, 16)], dz_t_in.at[k], sdt.at[k], rdt.at[k], stride(8 - k)))
    sum_i = dz_i[0:32, :]
    for cp in dsends:
        cp.wait()
    for p in range(1, 16):
        sum_i = sum_i + dz_i_in[p].astype(f32)
    swap_out[...] = sum_i[16:32, :]
    swap = send(swap_out, swap_in, sx.at[1], rx.at[1], pair)
    swap.wait()
    sum_i = sum_i[0:16, :] + swap_in[...]
    dots_i = jnp.sum(sum_i * unit_i, 1, keepdims=True)
    back[0, b2, b1, b0] = (inv_i * (sum_i - unit_i * dots_i)).astype(bf16)

    def spread(h, step):
        block = (
            back.at[h, b2, b1, b0] if step == 0 else back.at[h, :, b1, b0] if step == 1 else back.at[h, :, :, b0]
        )
        return send(block, block, sb.at[h, step], rb.at[h, step], (four, two, pair)[step])

    spreads = [spread(0, 0)]
    sum_t = dz_text[0:16, :]
    for cp in dtsends:
        cp.wait()
    for k in range(1, 8):
        sum_t = sum_t + dz_t_in[k].astype(f32)
    dots_t = jnp.sum(sum_t * unit_t, 1, keepdims=True)
    back[1, b2, b1, b0] = (inv_t * (sum_t - unit_t * dots_t)).astype(bf16)
    spreads.append(spread(1, 0))
    for step in (1, 2):
        for h in range(2):
            spreads[-2].wait_recv()
            spreads.append(spread(h, step))
    spreads[4].wait_recv()
    give = pl.ds(pl.multiple_of((1 - c) * 16, 16), 16)
    keep = pl.ds(pl.multiple_of(c * 16, 16), 16)
    halves = (pl.ds(0, 8), pl.ds(8, 8))
    grad_i[...] = dot(fi[...], back[0].reshape(128, E), ((0,), (0,)))
    for t in range(7):
        grads[t] = grad_i[pl.ds(pl.multiple_of(shift + 32 * t, 32), 32), :]
    grads[7] = jnp.zeros((32, E), f32)
    gsib = [send(grads.at[halves[0], give], grads_sib_in.at[halves[0]], sm.at[0], rm.at[0], sibling)]
    spreads[5].wait_recv()
    grads[8:16] = dot(ft[...], back[1].reshape(128, E), ((0,), (0,))).reshape(8, 32, E)
    gsib.append(send(grads.at[halves[1], give], grads_sib_in.at[halves[1]], sm.at[1], rm.at[1], sibling))
    for cp in spreads:
        cp.wait_send()

    def add_tile(t, carry):
        grads_wire[t] = (grads[t, keep, :] + grads_sib_in[t]).astype(grads_wire.dtype)
        return carry

    for h in range(2):
        gsib[h].wait()
        lax.fori_loop(8 * h, 8 * h + 8, add_tile, 0)
    me = plane_index(0)
    runs = (slice(0, 640), slice(640, E))
    spans = (pl.ds(0, 640), pl.ds(640, 512))
    gsends, zsends, osends, totals = [], [], [], []
    for h, cols in enumerate(spans):
        gsends.append([
            send(grads_wire.at[plane_index(p), :, cols], grads_in.at[p, :, cols], sg.at[h, p], rg.at[h, p], plane(p))
            for p in plane_order
        ])
    for h, run in enumerate(runs):
        total = grads[me, keep, run] + grads_sib_in[me, :, run]
        for cp in gsends[h]:
            cp.wait_recv()
        for p in range(1, 16):
            total = total + grads_in[p, :, run].astype(f32)
        zsum_out[:, run] = total
        zsends.append(send(zsum_out.at[:, spans[h]], zsum_in.at[:, spans[h]], sm.at[2 + h], rm.at[2 + h], far))
    for h, run in enumerate(runs):
        zsends[h].wait_recv()
        out[me, c, :, run] = (zsum_out[:, run] + zsum_in[:, run]).astype(out.dtype)
        tile = out.at[me, c, :, spans[h]]
        osends.append([send(tile, tile, so.at[h, p], ro.at[h, p], plane(p)) for p in plane_order])
    whole = []
    for h in range(2):
        for cp in osends[h]:
            cp.wait_recv()
        block = out.at[:, c, :, spans[h]]
        whole.append(send(block, block, sm.at[4 + h], rm.at[4 + h], sibling))
    for cp in gsends[0] + gsends[1] + zsends + osends[0] + osends[1]:
        cp.wait_send()
    for cp in whole:
        cp.wait()


def on_device(image_feats, text_feats, image_proj, text_proj, log_scale, logit_bias):
    dma = pltpu.SemaphoreType.DMA
    vmem = pltpu.VMEM
    wire_dz, wire_g, wire_o = bf16, bf16, bf16
    grads = pl.pallas_call(
        kernel,
        out_shape=jax.ShapeDtypeStruct((16, 2, 16, E), wire_o),
        in_specs=[pl.BlockSpec(memory_space=pl.ANY)] * 4 + [pl.BlockSpec(memory_space=pltpu.SMEM)] * 2,
        out_specs=pl.BlockSpec(memory_space=vmem),
        scratch_shapes=[
            vmem((128, 384), bf16), vmem((128, 256), bf16), vmem((384, E), bf16), vmem((256, E), bf16),
            vmem((2, 2, 2, 2, 16, E), f32), vmem((2, 2, 2, 2, 16, E), bf16),
            vmem((2, 2, 2, 16, E), f32), vmem((2, 2, 2, 16, E), bf16),
            vmem((2, 2, 16, E), f32),
            vmem((2, 2, 2, 16, E), bf16), vmem((2, 2, 16, E), bf16), vmem((2, 16, E), f32),
            vmem((512, E), bf16), vmem((256, E), bf16),
            vmem((32, E), f32), vmem((256, E), f32),
            vmem((512, E), wire_dz), vmem((16, 32, E), wire_dz),
            vmem((16, E), f32), vmem((16, E), f32),
            vmem((128, E), f32), vmem((128, E), wire_dz), vmem((8, 16, E), wire_dz),
            vmem((2, 2, 2, 2, 16, E), bf16), vmem((384, E), f32),
            vmem((16, 32, E), f32), vmem((16, 16, E), f32), vmem((16, 16, E), wire_g),
            vmem((16, 16, E), wire_g), vmem((16, E), f32), vmem((16, E), f32),
            dma((4,)), dma((2, 3)), dma((2, 3)), dma((8,)), dma((8,)), dma((2,)), dma((2,)), dma((9,)), dma((9,)),
            dma((2, 16)), dma((2, 16)), dma((16,)), dma((16,)), dma((8,)), dma((8,)),
            dma((2, 3)), dma((2, 3)), dma((2, 16)), dma((2, 16)), dma((2, 16)), dma((2, 16)), dma((6,)), dma((6,)), pltpu.SemaphoreType.REGULAR((3, 2)),
        ],
        compiler_params=pltpu.CompilerParams(
            collective_id=0, has_side_effects=True, vmem_limit_bytes=62 * 2**20
        ),
        name="heads",
    )(image_feats, text_feats, image_proj, text_proj, log_scale, logit_bias)
    grads = grads.reshape(512, E)
    return grads[:224].astype(f32), grads[256:].astype(f32)


def solution(mesh):
    placed = (P("dp", None), P("dp", None), P("mp", None), P("mp", None), P(), P())
    return jax.shard_map(
        on_device,
        mesh=mesh,
        in_specs=placed,
        out_specs=(P("mp", None), P("mp", None)),
        check_vma=False,
    )
```

```python
import jax
import jax.numpy as jnp
from jax import lax
from jax.experimental import pallas as pl
from jax.experimental.pallas import tpu as pltpu
from jax.sharding import PartitionSpec as P

norm_eps = 1e-06
f32, bf16 = jnp.float32, jnp.bfloat16
MESH = pl.DeviceIdType.MESH
E = 1152
plane_offsets = [(dx, dy) for dx in range(4) for dy in range(4)]
plane_order = sorted(range(1, 16), key=lambda p: -sum(min(o, 4 - o) for o in plane_offsets[p]))
line_order = [4, 3, 5, 2, 6, 1, 7]


def device_at(x, y, z, c):
    z_hi, z_lo = z // 8, lax.rem(z, 8)
    return {"dp": ((z_hi * 4 + y) * 4 + x) * 2 + c, "mp": z_lo}


def dot(a, b, dims):
    return lax.dot_general(a, b, (dims, ((), ())), preferred_element_type=f32)


def kernel(
    fi_hbm, ft_hbm, wi_hbm, wt_hbm, ls, lb, out,
    fi, ft, wi, wt, part, part_w, acc_1, acc_1w, acc_2, acc_2w, in_1, in_2, in_3,
    images, texts, dz_i, dz_t, dz_i_wire, dz_i_in, swap_out, swap_in,
    text_sib_in, dz_t_wire, dz_t_in, back, grad_i, grads, grads_sib_in, grads_wire,
    grads_in, zsum_out, zsum_in,
    sl, s1, r1, st, rt, sx, rx, ss, rs, si, ri, sdi, rdi, sdt, rdt, sb, rb, sg, rg, so, ro, sm, rm, gate,
):
    d, z_lo = lax.axis_index("dp"), lax.axis_index("mp")
    c, x, y, z_hi = lax.rem(d, 2), lax.rem(d // 2, 4), lax.rem(d // 8, 4), d // 32
    z = z_hi * 8 + z_lo
    b0, b1, b2 = lax.rem(z_lo, 2), lax.rem(z_lo // 2, 2), z_lo // 4
    sibling = device_at(x, y, z, 1 - c)
    pair = device_at(x, y, z + 1 - 2 * b0, c)
    two = device_at(x, y, z + 2 - 4 * b1, c)
    four = device_at(x, y, z + 4 - 8 * b2, c)
    far = device_at(x, y, lax.rem(z + 8, 16), c)

    def stride(k):
        return device_at(x, y, lax.rem(z + 2 * k, 16), c)

    def plane(p):
        dx, dy = plane_offsets[p]
        return device_at(lax.rem(x + dx, 4), lax.rem(y + dy, 4), z, c)

    def plane_back(p):
        dx, dy = plane_offsets[p]
        return device_at(lax.rem(x + 4 - dx, 4), lax.rem(y + 4 - dy, 4), z, c)

    def plane_index(p):
        dx, dy = plane_offsets[p]
        return lax.rem(x + dx, 4) * 4 + lax.rem(y + dy, 4)

    def send(src, dst, s, r, to):
        cp = pltpu.make_async_remote_copy(
            src_ref=src, dst_ref=dst, send_sem=s, recv_sem=r, device_id=to, device_id_type=MESH
        )
        cp.start()
        return cp

    def along(k):
        return device_at(x, y, lax.rem(z + 16 + k, 16), c)

    partners = [along(1), along(-1)] + [plane(p) for p in plane_order] + [sibling]
    barrier = pltpu.get_barrier_semaphore()
    for to in partners:
        pl.semaphore_signal(barrier, inc=1, device_id=to, device_id_type=MESH)

    def greet(r):
        pl.semaphore_signal(gate.at[r, 0], inc=1, device_id=along(2**r), device_id_type=MESH)
        pl.semaphore_signal(gate.at[r, 1], inc=1, device_id=along(-(2**r)), device_id_type=MESH)

    def greeted(r):
        pl.semaphore_wait(gate.at[r, 0], 1)
        pl.semaphore_wait(gate.at[r, 1], 1)

    window = pl.multiple_of(jnp.minimum(z_lo * 224 // 128 * 128, 1408), 128)
    shift = pl.multiple_of(z_lo * 224 - window, 32)
    wi[...] = jnp.zeros_like(wi)
    loads = [
        pltpu.make_async_copy(fi_hbm.at[:, pl.ds(window, 384)], fi, sl.at[0]),
        pltpu.make_async_copy(wi_hbm, wi.at[pl.ds(shift, 224)], sl.at[1]),
        pltpu.make_async_copy(ft_hbm.at[:, pl.ds(pl.multiple_of(z_lo * 256, 256), 256)], ft, sl.at[2]),
        pltpu.make_async_copy(wt_hbm, wt, sl.at[3]),
    ]
    for cp in loads:
        cp.start()
    for cp in loads[:2]:
        cp.wait()
    part[0] = dot(fi[...], wi[...], ((1,), (0,))).reshape(2, 2, 2, 16, E)
    part_w[0] = part[0].astype(bf16)
    for cp in loads[2:]:
        cp.wait()
    part[1] = dot(ft[...], wt[...], ((1,), (0,))).reshape(2, 2, 2, 16, E)
    part_w[1] = part[1].astype(bf16)
    pl.semaphore_wait(barrier, len(partners))
    greet(0)

    step_1 = [send(part_w.at[h, :, :, 1 - b0], in_1.at[h], s1.at[h, 0], r1.at[h, 0], pair) for h in range(2)]
    greeted(0)
    greet(1)
    step_2, step_3 = [], []
    for h in range(2):
        step_1[h].wait_recv()
        acc_1[h] = part[h, :, :, b0] + in_1[h].astype(f32)
        acc_1w[h] = acc_1[h].astype(bf16)
        step_2.append(send(acc_1w.at[h, :, 1 - b1], in_2.at[h], s1.at[h, 1], r1.at[h, 1], two))
    greeted(1)
    greet(2)
    for h in range(2):
        step_2[h].wait_recv()
        acc_2[h] = acc_1[h, :, b1] + in_2[h].astype(f32)
        acc_2w[h] = acc_2[h].astype(bf16)
        step_3.append(send(acc_2w.at[h, 1 - b2], in_3.at[h], s1.at[h, 2], r1.at[h, 2], four))

    step_3[0].wait_recv()
    pre_i = acc_2[0, b2] + in_3[0].astype(f32)
    inv_i = lax.rsqrt(jnp.sum(pre_i * pre_i, 1, keepdims=True) + norm_eps)
    unit_i = pre_i * inv_i
    images[0:16, :] = unit_i.astype(bf16)
    swap = send(images.at[pl.ds(0, 16)], images.at[pl.ds(16, 16)], sx.at[0], rx.at[0], pair)
    isends = []
    for p in plane_order:
        isends.append(send(images.at[pl.ds(0, 16)], images.at[pl.ds(32 * p, 16)], si.at[0, p], ri.at[0, p], plane(p)))
    step_3[1].wait_recv()
    pre_t = acc_2[1, b2] + in_3[1].astype(f32)
    inv_t = lax.rsqrt(jnp.sum(pre_t * pre_t, 1, keepdims=True) + norm_eps)
    unit_t = pre_t * inv_t
    texts[0:16, :] = unit_t.astype(bf16)
    greeted(2)
    tsends = {}
    for k in line_order:
        tsends[k] = send(texts.at[pl.ds(0, 16)], texts.at[pl.ds(16 * k, 16)], st.at[k], rt.at[k], stride(k))
    sib = [send(texts.at[pl.ds(0, 16)], texts.at[pl.ds(128, 16)], ss.at[0], rs.at[0], sibling)]
    swap.wait()
    for p in plane_order:
        isends.append(send(images.at[pl.ds(16, 16)], images.at[pl.ds(32 * p + 16, 16)], si.at[1, p], ri.at[1, p], plane(p)))
    for k in (1, 7, 2, 6, 3, 5, 4):
        tsends[k].wait()
        sib.append(send(texts.at[pl.ds(16 * k, 16)], texts.at[pl.ds(128 + 16 * k, 16)], ss.at[k], rs.at[k], sibling))
    for cp in sib + isends:
        cp.wait()
    for cp in step_1 + step_2 + step_3:
        cp.wait_send()

    scale = jnp.exp(jnp.full((8, 128), ls[0], f32))[0:1, 0:1]
    bias = lb[0]

    dsends = []
    for i in (2, 1, 3, 0):
        rows = slice(i * 128, i * 128 + 128)
        mine, every = images[rows, :], texts[...]
        logits = scale * dot(mine, every, ((1,), (1,))) + bias
        if i == 0:
            row = lax.broadcasted_iota(jnp.int32, (128, 256), 0)
            col = lax.broadcasted_iota(jnp.int32, (128, 256), 1)
            matched = (row == col) & (row < 16)
            sig = jax.nn.sigmoid(jnp.where(matched, -logits, logits))
            slopes = jnp.where(matched, -sig, sig)
        else:
            slopes = jax.nn.sigmoid(logits)
        weights = (scale * slopes).astype(bf16)
        dz_rows = dot(weights, every, ((1,), (0,)))
        if i == 0:
            dz_i[...] = dz_rows[0:32]
        dz_i_wire[rows, :] = dz_rows.astype(dz_i_wire.dtype)
        for p in plane_order:
            if p // 4 == i:
                dsends.append(send(dz_i_wire.at[pl.ds(32 * p, 32)], dz_i_in.at[p], sdi.at[p], rdi.at[p], plane_back(p)))
        more = dot(weights, mine, ((0,), (0,)))
        dz_t[...] = more if i == 2 else dz_t[...] + more

    tsib = send(dz_t.at[pl.ds(128, 128)], text_sib_in, ss.at[8], rs.at[8], sibling)
    tsib.wait()
    dz_text = dz_t[0:128, :] + text_sib_in[...]
    dz_t_wire[...] = dz_text.astype(dz_t_wire.dtype)
    dtsends = []
    for k in line_order:
        dtsends.append(send(dz_t_wire.at[pl.ds(16 * k, 16)], dz_t_in.at[k], sdt.at[k], rdt.at[k], stride(8 - k)))
    sum_i = dz_i[0:32, :]
    for cp in dsends:
        cp.wait()
    for p in range(1, 16):
        sum_i = sum_i + dz_i_in[p].astype(f32)
    swap_out[...] = sum_i[16:32, :]
    swap = send(swap_out, swap_in, sx.at[1], rx.at[1], pair)
    swap.wait()
    sum_i = sum_i[0:16, :] + swap_in[...]
    dots_i = jnp.sum(sum_i * unit_i, 1, keepdims=True)
    back[0, b2, b1, b0] = (inv_i * (sum_i - unit_i * dots_i)).astype(bf16)

    def spread(h, step):
        block = (
            back.at[h, b2, b1, b0] if step == 0 else back.at[h, :, b1, b0] if step == 1 else back.at[h, :, :, b0]
        )
        return send(block, block, sb.at[h, step], rb.at[h, step], (four, two, pair)[step])

    spreads = [spread(0, 0)]
    sum_t = dz_text[0:16, :]
    for cp in dtsends:
        cp.wait()
    for k in range(1, 8):
        sum_t = sum_t + dz_t_in[k].astype(f32)
    dots_t = jnp.sum(sum_t * unit_t, 1, keepdims=True)
    back[1, b2, b1, b0] = (inv_t * (sum_t - unit_t * dots_t)).astype(bf16)
    spreads.append(spread(1, 0))
    for step in (1, 2):
        for h in range(2):
            spreads[-2].wait_recv()
            spreads.append(spread(h, step))
    spreads[4].wait_recv()
    give = pl.ds(pl.multiple_of((1 - c) * 16, 16), 16)
    keep = pl.ds(pl.multiple_of(c * 16, 16), 16)
    halves = (pl.ds(0, 8), pl.ds(8, 8))
    grad_i[...] = dot(fi[...], back[0].reshape(128, E), ((0,), (0,)))
    for t in range(7):
        grads[t] = grad_i[pl.ds(pl.multiple_of(shift + 32 * t, 32), 32), :]
    grads[7] = jnp.zeros((32, E), f32)
    gsib = [send(grads.at[halves[0], give], grads_sib_in.at[halves[0]], sm.at[0], rm.at[0], sibling)]
    spreads[5].wait_recv()
    grads[8:16] = dot(ft[...], back[1].reshape(128, E), ((0,), (0,))).reshape(8, 32, E)
    gsib.append(send(grads.at[halves[1], give], grads_sib_in.at[halves[1]], sm.at[1], rm.at[1], sibling))
    for cp in spreads:
        cp.wait_send()

    def add_tile(t, carry):
        grads_wire[t] = (grads[t, keep, :] + grads_sib_in[t]).astype(grads_wire.dtype)
        return carry

    for h in range(2):
        gsib[h].wait()
        lax.fori_loop(8 * h, 8 * h + 8, add_tile, 0)
    me = plane_index(0)
    runs = (slice(0, 640), slice(640, E))
    spans = (pl.ds(0, 640), pl.ds(640, 512))
    gsends, zsends, osends, totals = [], [], [], []
    for h, cols in enumerate(spans):
        gsends.append([
            send(grads_wire.at[plane_index(p), :, cols], grads_in.at[p, :, cols], sg.at[h, p], rg.at[h, p], plane(p))
            for p in plane_order
        ])
    for h, run in enumerate(runs):
        total = grads[me, keep, run] + grads_sib_in[me, :, run]
        for cp in gsends[h]:
            cp.wait_recv()
        for p in range(1, 16):
            total = total + grads_in[p, :, run].astype(f32)
        zsum_out[:, run] = total
        zsends.append(send(zsum_out.at[:, spans[h]], zsum_in.at[:, spans[h]], sm.at[2 + h], rm.at[2 + h], far))
    for h, run in enumerate(runs):
        zsends[h].wait_recv()
        out[me, c, :, run] = (zsum_out[:, run] + zsum_in[:, run]).astype(out.dtype)
        tile = out.at[me, c, :, spans[h]]
        osends.append([send(tile, tile, so.at[h, p], ro.at[h, p], plane(p)) for p in plane_order])
    whole = []
    for h in range(2):
        for cp in osends[h]:
            cp.wait_recv()
        block = out.at[:, c, :, spans[h]]
        whole.append(send(block, block, sm.at[4 + h], rm.at[4 + h], sibling))
    for cp in gsends[0] + gsends[1] + zsends + osends[0] + osends[1]:
        cp.wait_send()
    for cp in whole:
        cp.wait()


def on_device(image_feats, text_feats, image_proj, text_proj, log_scale, logit_bias):
    dma = pltpu.SemaphoreType.DMA
    vmem = pltpu.VMEM
    wire_dz, wire_g, wire_o = bf16, f32, bf16
    grads = pl.pallas_call(
        kernel,
        out_shape=jax.ShapeDtypeStruct((16, 2, 16, E), wire_o),
        in_specs=[pl.BlockSpec(memory_space=pl.ANY)] * 4 + [pl.BlockSpec(memory_space=pltpu.SMEM)] * 2,
        out_specs=pl.BlockSpec(memory_space=vmem),
        scratch_shapes=[
            vmem((128, 384), bf16), vmem((128, 256), bf16), vmem((384, E), bf16), vmem((256, E), bf16),
            vmem((2, 2, 2, 2, 16, E), f32), vmem((2, 2, 2, 2, 16, E), bf16),
            vmem((2, 2, 2, 16, E), f32), vmem((2, 2, 2, 16, E), bf16),
            vmem((2, 2, 16, E), f32), vmem((2, 2, 16, E), bf16),
            vmem((2, 2, 2, 16, E), bf16), vmem((2, 2, 16, E), bf16), vmem((2, 16, E), bf16),
            vmem((512, E), bf16), vmem((256, E), bf16),
            vmem((32, E), f32), vmem((256, E), f32),
            vmem((512, E), wire_dz), vmem((16, 32, E), wire_dz),
            vmem((16, E), f32), vmem((16, E), f32),
            vmem((128, E), f32), vmem((128, E), wire_dz), vmem((8, 16, E), wire_dz),
            vmem((2, 2, 2, 2, 16, E), bf16), vmem((384, E), f32),
            vmem((16, 32, E), f32), vmem((16, 16, E), f32), vmem((16, 16, E), wire_g),
            vmem((16, 16, E), wire_g), vmem((16, E), f32), vmem((16, E), f32),
            dma((4,)), dma((2, 3)), dma((2, 3)), dma((8,)), dma((8,)), dma((2,)), dma((2,)), dma((9,)), dma((9,)),
            dma((2, 16)), dma((2, 16)), dma((16,)), dma((16,)), dma((8,)), dma((8,)),
            dma((2, 3)), dma((2, 3)), dma((2, 16)), dma((2, 16)), dma((2, 16)), dma((2, 16)), dma((6,)), dma((6,)), pltpu.SemaphoreType.REGULAR((3, 2)),
        ],
        compiler_params=pltpu.CompilerParams(
            collective_id=0, has_side_effects=True, vmem_limit_bytes=62 * 2**20
        ),
        name="heads",
    )(image_feats, text_feats, image_proj, text_proj, log_scale, logit_bias)
    grads = grads.reshape(512, E)
    return grads[:224].astype(f32), grads[256:].astype(f32)


def solution(mesh):
    placed = (P("dp", None), P("dp", None), P("mp", None), P("mp", None), P(), P())
    return jax.shard_map(
        on_device,
        mesh=mesh,
        in_specs=placed,
        out_specs=(P("mp", None), P("mp", None)),
        check_vma=False,
    )
```
